32 devices in a mesh: ctx: 8 (over z, x), fsdp: 4 (over y, core).
Axes of the slice: x: 2, y: 2, z: 4, core: 2. Of those that a mesh axis runs over, the one named last changes fastest.
Arguments:
- out_grad: bfloat16 [1024, 8192], P('ctx', 'fsdp'), may hold values from -6 to 6
- out_weight: bfloat16 [8192, 8192], P('ctx', 'fsdp'), may hold values from -0.0625 to 0.0625
- projections: bfloat16 [3, 1024, 8192], P(None, 'ctx', 'fsdp'), may hold values from -6 to 6
- short_filters: float32 [3, 3, 8192], P(None, None, 'fsdp'), may hold values from -3 to 3
- residues: float32 [16, 8192], P(None, 'fsdp'), may hold values from -0.06 to 0.06
- decay_rates: float32 [16, 8192], P(None, 'fsdp'), may hold values from 9.765625e-05 to 0.05
Outputs:
- grad_weight: bfloat16 [8192, 8192], P('ctx', 'fsdp')
- grad_projections: bfloat16 [3, 1024, 8192], P(None, 'ctx', 'fsdp')
- grad_short: float32 [3, 3, 8192], P(None, None, 'fsdp')
- grad_residues: float32 [16, 8192], P(None, 'fsdp')
- grad_rates: float32 [16, 8192], P(None, 'fsdp')
The draws below stay inside these ranges and needn't reach their ends.
All inputs are finite; a program needn't handle non-finite values.
Results may differ from the reference program's by a relative error of at most 0.005.
Values may be sent and summed in bfloat16 or wider, within the bound.
A program may use at most 192 MiB of HBM per device.

```python
import math
import jax
import jax.numpy as jnp
from jax import lax

D = 8192
SHORT = 3
N_MODES = 16
TOKENS = 1024


def strengthened(values, rng, source, target, blocks, factor):
    def block_of(dim):
        return (jnp.arange(values.shape[dim]) // (values.shape[dim] // blocks)).reshape((-1,) + (1,) * (values.ndim - 1 - dim))

    first = jax.random.permutation(rng, blocks)[block_of(target)]
    second = (block_of(target) + blocks // 2) % blocks
    return jnp.where((block_of(source) == first) | (block_of(source) == second), factor * values, values)


def levels(own_key, extent, cuts, least, largest):
    loudness = 1.0
    for dim, shards_of in cuts:
        draws = jax.random.uniform(jax.random.fold_in(jax.random.fold_in(own_key, 6), dim), (shards_of,), jnp.float32, least / len(cuts), largest / len(cuts))
        loudness = loudness * jnp.repeat(jnp.exp(draws), extent[dim] // shards_of).reshape((-1,) + (1,) * (len(extent) - 1 - dim))
    return loudness


def bell_draw(rng, extent, spread, most, cuts=(), held_as=jnp.bfloat16):
    values = jax.random.normal(rng, extent, jnp.float32) * spread
    if len(cuts) > 0:
        values = levels(rng, extent, cuts, -0.22, 0.18) * values
    return jnp.clip(values, min=-most, max=most).astype(held_as)


def noise_with(rng, shape, deviation, limit, cuts, heavy, dtype=jnp.bfloat16):
    result = deviation * jax.random.normal(rng, shape, jnp.float32)
    if cuts:
        result = result * levels(rng, shape, cuts, -0.22, 0.18)
    return jnp.clip(strengthened(result, jax.random.fold_in(rng, 3), *heavy), -limit, limit).astype(dtype)


def setup_inputs(seed: int = 0) -> dict:
    arg_keys = jax.random.split(jax.random.key(seed), 7)
    out_grad = noise_with(arg_keys[0], (TOKENS, D), 1.0, 6.0, ((0, 8), (1, 4)), (0, 1, 8, 2.0))
    out_weight = bell_draw(arg_keys[1], (D, D), D ** -0.5, 0.0625, ((0, 8), (1, 4)))
    projections = bell_draw(arg_keys[2], (3, TOKENS, D), 1.0, 6.0, ((1, 8), (2, 4)))
    short_filters = bell_draw(arg_keys[3], (3, SHORT, D), 0.5, 3.0, ((2, 4),), jnp.float32)
    residues = bell_draw(arg_keys[4], (N_MODES, D), 0.01, 0.06, ((1, 4),), jnp.float32)
    decay_rates = jnp.clip(jnp.exp(math.log(0.05) - 6.2383246 * jax.random.uniform(arg_keys[5], (N_MODES, D), jnp.float32) ** levels(arg_keys[5], (N_MODES, D), ((1, 4),), -0.2, 0.2)), 9.765625145519152e-05, 0.05)
    return dict(out_grad=out_grad, out_weight=out_weight, projections=projections, short_filters=short_filters, residues=residues, decay_rates=decay_rates)


def short_forward(padded, filters, length):
    total = filters[:, 0, None, :] * padded[:, SHORT - 1:SHORT - 1 + length, :]
    for offset in range(1, SHORT):
        total = total + filters[:, offset, None, :] * padded[:, SHORT - 1 - offset:SHORT - 1 - offset + length, :]
    return total


def channel_block(pieces):
    raw, filters, rates_block, residue_block, grad_y = pieces
    length = raw.shape[1]
    padded = jnp.pad(raw.astype(jnp.float32), ((0, 0), (SHORT - 1, 0), (0, 0)))
    branches = short_forward(padded, filters, length)
    q_branch, k_branch, v_branch = branches[0], branches[1], branches[2]
    product_kv = k_branch * v_branch
    decay = jnp.exp(-rates_block)

    def forward_step(state, value):
        state = decay * state + value[None, :]
        return state, state

    start_state = jnp.zeros(decay.shape, jnp.float32)
    _, states = lax.scan(forward_step, start_state, product_kv)
    long_out = jnp.sum(residue_block[None] * states, axis=1)
    y_rounded = (q_branch * long_out).astype(jnp.bfloat16)
    grad_long = grad_y * q_branch
    grad_q = grad_y * long_out

    def adjoint_step(state, value):
        state = decay * state + residue_block * value[None, :]
        return state, state

    _, adjoint = lax.scan(adjoint_step, start_state, grad_long, reverse=True)
    grad_kv = jnp.sum(adjoint, axis=1)
    grad_res = jnp.sum(grad_long[:, None, :] * states, axis=0)
    previous = jnp.concatenate([start_state[None], states[:-1]], axis=0)
    grad_rate = -decay * jnp.sum(adjoint * previous, axis=0)
    grad_branches = jnp.stack([grad_q, grad_kv * v_branch, grad_kv * k_branch])
    padded_back = jnp.pad(grad_branches, ((0, 0), (0, SHORT - 1), (0, 0)))
    grad_raw = filters[:, 0, None, :] * padded_back[:, 0:length, :]
    filter_terms = [jnp.sum(grad_branches * padded[:, SHORT - 1:SHORT - 1 + length, :], axis=1)]
    for offset in range(1, SHORT):
        grad_raw = grad_raw + filters[:, offset, None, :] * padded_back[:, offset:offset + length, :]
        filter_terms.append(jnp.sum(grad_branches * padded[:, SHORT - 1 - offset:SHORT - 1 - offset + length, :], axis=1))
    grad_filters = jnp.stack(filter_terms, axis=1)
    return grad_raw.astype(jnp.bfloat16), grad_filters, grad_res, grad_rate, y_rounded


def reference(out_grad, out_weight, projections, short_filters, residues, decay_rates):
    grad_y = jnp.dot(out_grad, out_weight, preferred_element_type=jnp.float32)
    width = math.gcd(D, 512)
    blocks = D // width

    def split(array):
        shaped = array.reshape(array.shape[:-1] + (blocks, width))
        return jnp.moveaxis(shaped, -2, 0)

    def join(array):
        moved = jnp.moveaxis(array, 0, -2)
        return moved.reshape(moved.shape[:-2] + (D,))

    pieces = (split(projections), split(short_filters), split(decay_rates), split(residues), split(grad_y))
    grad_raw, grad_filters, grad_res, grad_rate, y_rounded = lax.map(channel_block, pieces)
    grad_weight = lax.dot_general(out_grad, join(y_rounded), (((0,), (0,)), ((), ())), preferred_element_type=jnp.float32)
    return grad_weight.astype(jnp.bfloat16), join(grad_raw), join(grad_filters), join(grad_res), join(grad_rate)
```

```python
import math

import jax
import jax.numpy as jnp
from jax import lax
from jax.experimental import pallas as pl
from jax.experimental.pallas import tpu as pltpu
from jax.sharding import PartitionSpec as P

CHUNKS = 8
GROUP = 8


def pair_sum(terms):
    while len(terms) > 1:
        paired = [a + b for a, b in zip(terms[0::2], terms[1::2])]
        terms = paired + ([terms[-1]] if len(terms) % 2 else [])
    return terms[0]


def spread(ref, modes, lanes):
    return [jnp.broadcast_to(ref[n], (CHUNKS, lanes)) for n in modes]


def forward_kernel(kv_ref, decay_ref, jump_ref, res_ref, long_ref, entry_ref, final_ref):
    steps, _, lanes = kv_ref.shape
    modes = range(decay_ref.shape[0])
    decay = spread(decay_ref, modes, lanes)
    zeros = [jnp.zeros((CHUNKS, lanes), jnp.float32) for _ in modes]

    def finals(r, state):
        x = kv_ref[r]
        return [d * s + x for d, s in zip(decay, state)]

    state = lax.fori_loop(0, steps, finals, zeros, unroll=4)
    for n in modes:
        final_ref[n] = state[n]
    jump = jump_ref[...]
    entering = jnp.zeros_like(jump)
    for c in range(CHUNKS):
        entry_ref[:, c : c + 1, :] = entering
        entering = jump * entering + final_ref[:, c : c + 1, :]
    res = spread(res_ref, modes, lanes)

    def outputs(r, state):
        x = kv_ref[r]
        state = [d * s + x for d, s in zip(decay, state)]
        long_ref[r] = pair_sum([w * s for w, s in zip(res, state)])
        return state

    lax.fori_loop(0, steps, outputs, [entry_ref[n] for n in modes], unroll=4)


def backward_kernel(
    kv_ref, gl_ref, decay_ref, jump_ref, res_ref, entry_ref,
    gkv_ref, gres_ref, grate_ref, prev_ref, final_ref, enter_ref,
):
    steps, _, lanes = kv_ref.shape
    n_modes = decay_ref.shape[0]
    modes = range(n_modes)
    decay = spread(decay_ref, modes, lanes)
    zeros = [jnp.zeros((CHUNKS, lanes), jnp.float32) for _ in modes]

    def first(r, carry):
        state, adjoint = carry
        x = kv_ref[r]
        g = gl_ref[steps - 1 - r]
        for n in modes:
            prev_ref[r, n] = state[n]
        return (
            [d * s + x for d, s in zip(decay, state)],
            [d * a + g for d, a in zip(decay, adjoint)],
        )

    _, adjoint = lax.fori_loop(0, steps, first, ([entry_ref[n] for n in modes], zeros), unroll=2)
    for n in modes:
        final_ref[n] = adjoint[n]
    jump = jump_ref[...]
    entering = jnp.zeros_like(jump)
    for c in reversed(range(CHUNKS)):
        enter_ref[:, c : c + 1, :] = entering
        entering = jump * entering + final_ref[:, c : c + 1, :]

    for start in range(0, n_modes, GROUP):
        group = range(start, min(start + GROUP, n_modes))
        d_group = spread(decay_ref, group, lanes)
        r_group = spread(res_ref, group, lanes)
        zero = [jnp.zeros((CHUNKS, lanes), jnp.float32) for _ in group]

        def second(k, carry, start=start, group=group, d_group=d_group, r_group=r_group):
            adjoint, res_sum, rate_sum = carry
            r = steps - 1 - k
            g = gl_ref[r]
            x = kv_ref[r]
            adjoint = [d * a + g for d, a in zip(d_group, adjoint)]
            total = pair_sum([w * a for w, a in zip(r_group, adjoint)])
            gkv_ref[r] = total if start == 0 else gkv_ref[r] + total
            res_sum = [s + a * x for s, a in zip(res_sum, adjoint)]
            rate_sum = [s + a * prev_ref[r, n] for s, a, n in zip(rate_sum, adjoint, group)]
            return adjoint, res_sum, rate_sum

        _, res_sum, rate_sum = lax.fori_loop(
            0, steps, second, ([enter_ref[n] for n in group], zero, zero), unroll=2
        )
        for k, n in enumerate(group):
            gres_ref[n] = jnp.sum(res_sum[k], axis=0, keepdims=True)
            grate_ref[n] = (
                -decay_ref[n] * res_ref[n] * jnp.sum(rate_sum[k], axis=0, keepdims=True)
            )


def series_spec(steps, lanes):
    return pl.BlockSpec((steps, CHUNKS, lanes), lambda b: (0, 0, b))


def mode_spec(n_modes, rows, lanes):
    return pl.BlockSpec((n_modes, rows, lanes), lambda b: (0, 0, b))


def run_forward(kv, decay, jump, res):
    steps, _, width = kv.shape
    n_modes = decay.shape[0]
    lanes = math.gcd(width, 128)
    series, row = series_spec(steps, lanes), mode_spec(n_modes, 1, lanes)
    return pl.pallas_call(
        forward_kernel,
        grid=(width // lanes,),
        in_specs=[series, row, row, row],
        out_specs=[series, mode_spec(n_modes, CHUNKS, lanes)],
        out_shape=[
            jax.ShapeDtypeStruct(kv.shape, jnp.float32),
            jax.ShapeDtypeStruct((n_modes, CHUNKS, width), jnp.float32),
        ],
        scratch_shapes=[pltpu.VMEM((n_modes, CHUNKS, lanes), jnp.float32)],
        compiler_params=pltpu.CompilerParams(vmem_limit_bytes=32 * 2**20),
        cost_estimate=pl.CostEstimate(
            flops=6 * kv.size * n_modes, bytes_accessed=8 * kv.size, transcendentals=0
        ),
    )(kv, decay, jump, res)


def run_backward(kv, gl, decay, jump, res, entry):
    steps, _, width = kv.shape
    n_modes = decay.shape[0]
    lanes = math.gcd(width, 128)
    series, row = series_spec(steps, lanes), mode_spec(n_modes, 1, lanes)
    carried = mode_spec(n_modes, CHUNKS, lanes)
    return pl.pallas_call(
        backward_kernel,
        grid=(width // lanes,),
        in_specs=[series, series, row, row, row, carried],
        out_specs=[series, row, row],
        out_shape=[
            jax.ShapeDtypeStruct(kv.shape, jnp.float32),
            jax.ShapeDtypeStruct(decay.shape, jnp.float32),
            jax.ShapeDtypeStruct(decay.shape, jnp.float32),
        ],
        scratch_shapes=[
            pltpu.VMEM((steps, n_modes, CHUNKS, lanes), jnp.float32),
            pltpu.VMEM((n_modes, CHUNKS, lanes), jnp.float32),
            pltpu.VMEM((n_modes, CHUNKS, lanes), jnp.float32),
        ],
        compiler_params=pltpu.CompilerParams(vmem_limit_bytes=44 * 2**20),
        cost_estimate=pl.CostEstimate(
            flops=12 * kv.size * n_modes, bytes_accessed=12 * kv.size, transcendentals=0
        ),
    )(kv, gl, decay, jump, res, entry)


def to_chunks(series):
    length, width = series.shape
    return jnp.swapaxes(series.reshape(CHUNKS, length // CHUNKS, width), 0, 1)


def from_chunks(series):
    steps, _, width = series.shape
    return jnp.swapaxes(series, 0, 1).reshape(CHUNKS * steps, width)


def on_device(out_grad, out_weight, projections, short_filters, residues, decay_rates):
    devices, index = lax.axis_size("ctx"), lax.axis_index("ctx")
    panels = lax.axis_size("fsdp")
    tokens, wide = out_grad.shape
    length = tokens * devices
    share = projections.shape[2] // devices

    series = lax.all_to_all(projections, "ctx", split_axis=2, concat_axis=1, tiled=True)

    rows = tokens // panels
    mine = lax.all_to_all(out_grad, "fsdp", split_axis=0, concat_axis=1, tiled=True)
    mine = lax.all_to_all(mine, "ctx", split_axis=1, concat_axis=0, tiled=True)
    mine = lax.all_gather(mine.reshape(devices, rows, -1), "fsdp", axis=1)
    cotangent = mine.reshape(length, -1)

    def own(array):
        return lax.dynamic_slice_in_dim(array, index * share, share, axis=array.ndim - 1)

    filters, res, rates = own(short_filters), own(residues), own(decay_rates)
    taps = filters.shape[1]
    margin = taps - 1
    steps = length // CHUNKS
    decay = jnp.exp(-rates)[:, None, :]
    jump = jnp.exp(-rates * float(steps))[:, None, :]
    res = res[:, None, :]

    extended = jnp.pad(series, ((0, 0), (margin, 0), (0, 0))).astype(jnp.float32)
    delayed = [extended[:, margin - j : margin - j + length, :] for j in range(taps)]
    branches = sum(filters[:, j, None, :] * delayed[j] for j in range(taps))
    q_branch, k_branch, v_branch = branches[0], branches[1], branches[2]
    kv = to_chunks(k_branch * v_branch)
    long_chunks, entry = run_forward(kv, decay, jump, res)
    long_out = from_chunks(long_chunks)
    y_rounded = (q_branch * long_out).astype(jnp.bfloat16)
    y_all = lax.all_gather(y_rounded, "ctx", axis=1, tiled=True)

    partial = jnp.dot(cotangent, out_weight, preferred_element_type=jnp.float32)
    partial = partial.astype(jnp.bfloat16).reshape(length, devices, share)
    partial = lax.all_to_all(partial, "ctx", split_axis=1, concat_axis=0)
    grad_y = jnp.sum(partial.astype(jnp.float32), axis=0)

    grad_weight = lax.dot_general(
        cotangent, y_all, (((0,), (0,)), ((), ())), preferred_element_type=jnp.float32
    ).astype(jnp.bfloat16)

    gkv_chunks, grad_res, grad_rate = run_backward(
        kv, to_chunks(grad_y * q_branch), decay, jump, res, entry
    )
    grad_kv = from_chunks(gkv_chunks)
    grad_branches = jnp.stack([grad_y * long_out, grad_kv * v_branch, grad_kv * k_branch])
    extended_back = jnp.pad(grad_branches, ((0, 0), (0, margin), (0, 0)))
    grad_raw = sum(
        filters[:, j, None, :] * extended_back[:, j : j + length, :] for j in range(taps)
    ).astype(jnp.bfloat16)
    grad_raw = lax.all_to_all(grad_raw, "ctx", split_axis=1, concat_axis=2, tiled=True)
    grad_short = jnp.stack(
        [jnp.sum(grad_branches * delayed[j], axis=1) for j in range(taps)], axis=1
    )

    n_short, n_modes = 3 * taps, res.shape[0]
    small = jnp.concatenate(
        [grad_short.reshape(n_short, share), grad_res[:, 0, :], grad_rate[:, 0, :]]
    )
    small = lax.all_gather(small, "ctx", axis=1, tiled=True)
    return (
        grad_weight,
        grad_raw,
        small[:n_short].reshape(3, taps, -1),
        small[n_short : n_short + n_modes],
        small[n_short + n_modes :],
    )


def solution(mesh):
    placed = (
        P("ctx", "fsdp"),
        P("ctx", "fsdp"),
        P(None, "ctx", "fsdp"),
        P(None, None, "fsdp"),
        P(None, "fsdp"),
        P(None, "fsdp"),
    )
    return jax.shard_map(
        on_device,
        mesh=mesh,
        in_specs=placed,
        out_specs=(
            P("ctx", "fsdp"),
            P(None, "ctx", "fsdp"),
            P(None, None, "fsdp"),
            P(None, "fsdp"),
            P(None, "fsdp"),
        ),
        check_vma=False,
    )
```

```python
import math

import jax
import jax.numpy as jnp
from jax import lax
from jax.experimental import pallas as pl
from jax.experimental.pallas import tpu as pltpu
from jax.sharding import PartitionSpec as P

CHUNKS = 8
GROUP = 8


def pair_sum(terms):
    while len(terms) > 1:
        paired = [a + b for a, b in zip(terms[0::2], terms[1::2])]
        terms = paired + ([terms[-1]] if len(terms) % 2 else [])
    return terms[0]


def spread(ref, modes, lanes):
    return [jnp.broadcast_to(ref[n], (CHUNKS, lanes)) for n in modes]


def forward_kernel(kv_ref, decay_ref, jump_ref, res_ref, long_ref, entry_ref, final_ref):
    steps, _, lanes = kv_ref.shape
    modes = range(decay_ref.shape[0])
    decay = spread(decay_ref, modes, lanes)
    zeros = [jnp.zeros((CHUNKS, lanes), jnp.float32) for _ in modes]

    def finals(r, state):
        x = kv_ref[r]
        return [d * s + x for d, s in zip(decay, state)]

    state = lax.fori_loop(0, steps, finals, zeros, unroll=4)
    for n in modes:
        final_ref[n] = state[n]
    jump = jump_ref[...]
    entering = jnp.zeros_like(jump)
    for c in range(CHUNKS):
        entry_ref[:, c : c + 1, :] = entering
        entering = jump * entering + final_ref[:, c : c + 1, :]
    res = spread(res_ref, modes, lanes)

    def outputs(r, state):
        x = kv_ref[r]
        state = [d * s + x for d, s in zip(decay, state)]
        long_ref[r] = pair_sum([w * s for w, s in zip(res, state)])
        return state

    lax.fori_loop(0, steps, outputs, [entry_ref[n] for n in modes], unroll=4)


def backward_kernel(
    kv_ref, gl_ref, decay_ref, jump_ref, res_ref, entry_ref,
    gkv_ref, gres_ref, grate_ref, prev_ref, final_ref, enter_ref,
):
    steps, _, lanes = kv_ref.shape
    n_modes = decay_ref.shape[0]
    modes = range(n_modes)
    decay = spread(decay_ref, modes, lanes)
    zeros = [jnp.zeros((CHUNKS, lanes), jnp.float32) for _ in modes]

    def first(r, carry):
        state, adjoint = carry
        x = kv_ref[r]
        g = gl_ref[steps - 1 - r]
        for n in modes:
            prev_ref[r, n] = state[n]
        return (
            [d * s + x for d, s in zip(decay, state)],
            [d * a + g for d, a in zip(decay, adjoint)],
        )

    _, adjoint = lax.fori_loop(0, steps, first, ([entry_ref[n] for n in modes], zeros), unroll=2)
    for n in modes:
        final_ref[n] = adjoint[n]
    jump = jump_ref[...]
    entering = jnp.zeros_like(jump)
    for c in reversed(range(CHUNKS)):
        enter_ref[:, c : c + 1, :] = entering
        entering = jump * entering + final_ref[:, c : c + 1, :]

    for start in range(0, n_modes, GROUP):
        group = range(start, min(start + GROUP, n_modes))
        d_group = spread(decay_ref, group, lanes)
        r_group = spread(res_ref, group, lanes)
        zero = [jnp.zeros((CHUNKS, lanes), jnp.float32) for _ in group]

        def second(k, carry, start=start, group=group, d_group=d_group, r_group=r_group):
            adjoint, res_sum, rate_sum = carry
            r = steps - 1 - k
            g = gl_ref[r]
            x = kv_ref[r]
            adjoint = [d * a + g for d, a in zip(d_group, adjoint)]
            total = pair_sum([w * a for w, a in zip(r_group, adjoint)])
            gkv_ref[r] = total if start == 0 else gkv_ref[r] + total
            res_sum = [s + a * x for s, a in zip(res_sum, adjoint)]
            rate_sum = [s + a * prev_ref[r, n] for s, a, n in zip(rate_sum, adjoint, group)]
            return adjoint, res_sum, rate_sum

        _, res_sum, rate_sum = lax.fori_loop(
            0, steps, second, ([enter_ref[n] for n in group], zero, zero), unroll=2
        )
        for k, n in enumerate(group):
            gres_ref[n] = jnp.sum(res_sum[k], axis=0, keepdims=True)
            grate_ref[n] = (
                -decay_ref[n] * res_ref[n] * jnp.sum(rate_sum[k], axis=0, keepdims=True)
            )


def series_spec(steps, lanes):
    return pl.BlockSpec((steps, CHUNKS, lanes), lambda b: (0, 0, b))


def mode_spec(n_modes, rows, lanes):
    return pl.BlockSpec((n_modes, rows, lanes), lambda b: (0, 0, b))


def run_forward(kv, decay, jump, res):
    steps, _, width = kv.shape
    n_modes = decay.shape[0]
    lanes = math.gcd(width, 128)
    series, row = series_spec(steps, lanes), mode_spec(n_modes, 1, lanes)
    return pl.pallas_call(
        forward_kernel,
        grid=(width // lanes,),
        in_specs=[series, row, row, row],
        out_specs=[series, mode_spec(n_modes, CHUNKS, lanes)],
        out_shape=[
            jax.ShapeDtypeStruct(kv.shape, jnp.float32),
            jax.ShapeDtypeStruct((n_modes, CHUNKS, width), jnp.float32),
        ],
        scratch_shapes=[pltpu.VMEM((n_modes, CHUNKS, lanes), jnp.float32)],
        compiler_params=pltpu.CompilerParams(vmem_limit_bytes=32 * 2**20),
        cost_estimate=pl.CostEstimate(
            flops=6 * kv.size * n_modes, bytes_accessed=8 * kv.size, transcendentals=0
        ),
    )(kv, decay, jump, res)


def run_backward(kv, gl, decay, jump, res, entry):
    steps, _, width = kv.shape
    n_modes = decay.shape[0]
    lanes = math.gcd(width, 128)
    series, row = series_spec(steps, lanes), mode_spec(n_modes, 1, lanes)
    carried = mode_spec(n_modes, CHUNKS, lanes)
    return pl.pallas_call(
        backward_kernel,
        grid=(width // lanes,),
        in_specs=[series, series, row, row, row, carried],
        out_specs=[series, row, row],
        out_shape=[
            jax.ShapeDtypeStruct(kv.shape, jnp.float32),
            jax.ShapeDtypeStruct(decay.shape, jnp.float32),
            jax.ShapeDtypeStruct(decay.shape, jnp.float32),
        ],
        scratch_shapes=[
            pltpu.VMEM((steps, n_modes, CHUNKS, lanes), jnp.float32),
            pltpu.VMEM((n_modes, CHUNKS, lanes), jnp.float32),
            pltpu.VMEM((n_modes, CHUNKS, lanes), jnp.float32),
        ],
        compiler_params=pltpu.CompilerParams(vmem_limit_bytes=44 * 2**20),
        cost_estimate=pl.CostEstimate(
            flops=12 * kv.size * n_modes, bytes_accessed=12 * kv.size, transcendentals=0
        ),
    )(kv, gl, decay, jump, res, entry)


def to_chunks(series):
    length, width = series.shape
    return jnp.swapaxes(series.reshape(CHUNKS, length // CHUNKS, width), 0, 1)


def from_chunks(series):
    steps, _, width = series.shape
    return jnp.swapaxes(series, 0, 1).reshape(CHUNKS * steps, width)


def on_device(out_grad, out_weight, projections, short_filters, residues, decay_rates):
    devices, index = lax.axis_size("ctx"), lax.axis_index("ctx")
    panels = lax.axis_size("fsdp")
    tokens, wide = out_grad.shape
    length = tokens * devices
    share = projections.shape[2] // devices

    series = lax.all_to_all(projections, "ctx", split_axis=2, concat_axis=1, tiled=True)

    rows = tokens // panels
    mine = lax.all_to_all(out_grad, "fsdp", split_axis=0, concat_axis=1, tiled=True)
    mine = lax.all_to_all(mine, "ctx", split_axis=1, concat_axis=0, tiled=True)
    mine = lax.all_gather(mine.reshape(devices, rows, -1), "fsdp", axis=1)
    cotangent = mine.reshape(length, -1)

    def own(array):
        return lax.dynamic_slice_in_dim(array, index * share, share, axis=array.ndim - 1)

    filters, res, rates = own(short_filters), own(residues), own(decay_rates)
    taps = filters.shape[1]
    margin = taps - 1
    steps = length // CHUNKS
    decay = jnp.exp(-rates)[:, None, :]
    jump = jnp.exp(-rates * float(steps))[:, None, :]
    res = res[:, None, :]

    extended = jnp.pad(series, ((0, 0), (margin, 0), (0, 0))).astype(jnp.float32)
    delayed = [extended[:, margin - j : margin - j + length, :] for j in range(taps)]
    branches = sum(filters[:, j, None, :] * delayed[j] for j in range(taps))
    q_branch, k_branch, v_branch = branches[0], branches[1], branches[2]
    kv = to_chunks(k_branch * v_branch)
    long_chunks, entry = run_forward(kv, decay, jump, res)
    long_out = from_chunks(long_chunks)
    y_rounded = (q_branch * long_out).astype(jnp.bfloat16)
    y_all = lax.all_gather(y_rounded, "ctx", axis=1, tiled=True)

    outer, side = devices // 2, lax.rem(index, 2)
    paired = out_weight.reshape(out_weight.shape[0], outer, 2, share)

    def half(which):
        columns = lax.dynamic_index_in_dim(paired, which, axis=2, keepdims=False)
        return columns.reshape(-1, outer * share)

    swap = [(i, i ^ 1) for i in range(devices)]
    lanes_of = [[2 * z + x for z in range(outer)] for x in range(2)]
    theirs, ours = half(1 - side), half(side)
    pieces = []
    for piece in jnp.split(cotangent, 2, axis=0):
        sent = jnp.dot(piece, theirs, preferred_element_type=jnp.float32)
        other = lax.ppermute(sent.astype(jnp.bfloat16), "ctx", swap)
        kept = jnp.dot(piece, ours, preferred_element_type=jnp.float32)
        both = (kept + other.astype(jnp.float32)).astype(jnp.bfloat16)
        terms = lax.all_to_all(
            both.reshape(-1, outer, share), "ctx", 1, 0, axis_index_groups=lanes_of
        )
        pieces.append(jnp.sum(terms.astype(jnp.float32), axis=0))
    grad_y = jnp.concatenate(pieces, axis=0)

    grad_weight = lax.dot_general(
        cotangent, y_all, (((0,), (0,)), ((), ())), preferred_element_type=jnp.float32
    ).astype(jnp.bfloat16)

    gkv_chunks, grad_res, grad_rate = run_backward(
        kv, to_chunks(grad_y * q_branch), decay, jump, res, entry
    )
    grad_kv = from_chunks(gkv_chunks)
    grad_branches = jnp.stack([grad_y * long_out, grad_kv * v_branch, grad_kv * k_branch])
    extended_back = jnp.pad(grad_branches, ((0, 0), (0, margin), (0, 0)))
    grad_raw = sum(
        filters[:, j, None, :] * extended_back[:, j : j + length, :] for j in range(taps)
    ).astype(jnp.bfloat16)
    grad_short = jnp.stack(
        [jnp.sum(grad_branches * delayed[j], axis=1) for j in range(taps)], axis=1
    )

    n_short, n_modes = 3 * taps, res.shape[0]
    small = jnp.concatenate(
        [grad_short.reshape(n_short, share), grad_res[:, 0, :], grad_rate[:, 0, :]]
    )
    small = jnp.pad(small, ((0, -small.shape[0] % 16), (0, 0)))
    padded = small.shape[0]
    high = lax.reduce_precision(small, 8, 7)
    parts = jnp.concatenate([high, small - high]).astype(jnp.bfloat16)
    own_rows = 3 * tokens
    sent = jnp.swapaxes(grad_raw.reshape(3, devices, tokens, share), 0, 1)
    sent = jnp.concatenate(
        [
            sent.reshape(devices, own_rows, share),
            jnp.broadcast_to(parts[None], (devices,) + parts.shape),
        ],
        axis=1,
    )
    got = lax.all_to_all(sent, "ctx", 0, 0)
    grad_raw = got[:, :own_rows].reshape(devices, 3, tokens, share)
    grad_raw = jnp.transpose(grad_raw, (1, 2, 0, 3)).reshape(3, tokens, -1)
    low = got[:, own_rows + padded :].astype(jnp.float32)
    small = got[:, own_rows : own_rows + padded].astype(jnp.float32) + low
    small = jnp.swapaxes(small, 0, 1).reshape(padded, -1)
    return (
        grad_weight,
        grad_raw,
        small[:n_short].reshape(3, taps, -1),
        small[n_short : n_short + n_modes],
        small[n_short + n_modes : n_short + 2 * n_modes],
    )


def solution(mesh):
    placed = (
        P("ctx", "fsdp"),
        P("ctx", "fsdp"),
        P(None, "ctx", "fsdp"),
        P(None, None, "fsdp"),
        P(None, "fsdp"),
        P(None, "fsdp"),
    )
    return jax.shard_map(
        on_device,
        mesh=mesh,
        in_specs=placed,
        out_specs=(
            P("ctx", "fsdp"),
            P(None, "ctx", "fsdp"),
            P(None, None, "fsdp"),
            P(None, "fsdp"),
            P(None, "fsdp"),
        ),
        check_vma=False,
    )
```

```python
import math

import jax
import jax.numpy as jnp
from jax import lax
from jax.experimental import pallas as pl
from jax.experimental.pallas import tpu as pltpu
from jax.sharding import PartitionSpec as P

CHUNKS = 8
GROUP = 8


def pair_sum(terms):
    while len(terms) > 1:
        paired = [a + b for a, b in zip(terms[0::2], terms[1::2])]
        terms = paired + ([terms[-1]] if len(terms) % 2 else [])
    return terms[0]


def spread(ref, modes, lanes):
    return [jnp.broadcast_to(ref[n], (CHUNKS, lanes)) for n in modes]


def forward_kernel(kv_ref, decay_ref, jump_ref, res_ref, long_ref, entry_ref, final_ref):
    steps, _, lanes = kv_ref.shape
    modes = range(decay_ref.shape[0])
    decay = spread(decay_ref, modes, lanes)
    zeros = [jnp.zeros((CHUNKS, lanes), jnp.float32) for _ in modes]

    def finals(r, state):
        x = kv_ref[r]
        return [d * s + x for d, s in zip(decay, state)]

    state = lax.fori_loop(0, steps, finals, zeros, unroll=4)
    for n in modes:
        final_ref[n] = state[n]
    jump = jump_ref[...]
    entering = jnp.zeros_like(jump)
    for c in range(CHUNKS):
        entry_ref[:, c : c + 1, :] = entering
        entering = jump * entering + final_ref[:, c : c + 1, :]
    res = spread(res_ref, modes, lanes)

    def outputs(r, state):
        x = kv_ref[r]
        state = [d * s + x for d, s in zip(decay, state)]
        long_ref[r] = pair_sum([w * s for w, s in zip(res, state)])
        return state

    lax.fori_loop(0, steps, outputs, [entry_ref[n] for n in modes], unroll=4)


def backward_kernel(
    kv_ref, gl_ref, decay_ref, jump_ref, res_ref, entry_ref,
    gkv_ref, gres_ref, grate_ref, prev_ref, final_ref, enter_ref,
):
    steps, _, lanes = kv_ref.shape
    n_modes = decay_ref.shape[0]
    modes = range(n_modes)
    decay = spread(decay_ref, modes, lanes)
    zeros = [jnp.zeros((CHUNKS, lanes), jnp.float32) for _ in modes]

    def first(r, carry):
        state, adjoint = carry
        x = kv_ref[r]
        g = gl_ref[steps - 1 - r]
        for n in modes:
            prev_ref[r, n] = state[n]
        return (
            [d * s + x for d, s in zip(decay, state)],
            [d * a + g for d, a in zip(decay, adjoint)],
        )

    _, adjoint = lax.fori_loop(0, steps, first, ([entry_ref[n] for n in modes], zeros), unroll=2)
    for n in modes:
        final_ref[n] = adjoint[n]
    jump = jump_ref[...]
    entering = jnp.zeros_like(jump)
    for c in reversed(range(CHUNKS)):
        enter_ref[:, c : c + 1, :] = entering
        entering = jump * entering + final_ref[:, c : c + 1, :]

    for start in range(0, n_modes, GROUP):
        group = range(start, min(start + GROUP, n_modes))
        d_group = spread(decay_ref, group, lanes)
        r_group = spread(res_ref, group, lanes)
        zero = [jnp.zeros((CHUNKS, lanes), jnp.float32) for _ in group]

        def second(k, carry, start=start, group=group, d_group=d_group, r_group=r_group):
            adjoint, res_sum, rate_sum = carry
            r = steps - 1 - k
            g = gl_ref[r]
            x = kv_ref[r]
            adjoint = [d * a + g for d, a in zip(d_group, adjoint)]
            total = pair_sum([w * a for w, a in zip(r_group, adjoint)])
            gkv_ref[r] = total if start == 0 else gkv_ref[r] + total
            res_sum = [s + a * x for s, a in zip(res_sum, adjoint)]
            rate_sum = [s + a * prev_ref[r, n] for s, a, n in zip(rate_sum, adjoint, group)]
            return adjoint, res_sum, rate_sum

        _, res_sum, rate_sum = lax.fori_loop(
            0, steps, second, ([enter_ref[n] for n in group], zero, zero), unroll=2
        )
        for k, n in enumerate(group):
            gres_ref[n] = jnp.sum(res_sum[k], axis=0, keepdims=True)
            grate_ref[n] = (
                -decay_ref[n] * res_ref[n] * jnp.sum(rate_sum[k], axis=0, keepdims=True)
            )


def series_spec(steps, lanes):
    return pl.BlockSpec((steps, CHUNKS, lanes), lambda b: (0, 0, b))


def mode_spec(n_modes, rows, lanes):
    return pl.BlockSpec((n_modes, rows, lanes), lambda b: (0, 0, b))


def run_forward(kv, decay, jump, res):
    steps, _, width = kv.shape
    n_modes = decay.shape[0]
    lanes = math.gcd(width, 128)
    series, row = series_spec(steps, lanes), mode_spec(n_modes, 1, lanes)
    return pl.pallas_call(
        forward_kernel,
        grid=(width // lanes,),
        in_specs=[series, row, row, row],
        out_specs=[series, mode_spec(n_modes, CHUNKS, lanes)],
        out_shape=[
            jax.ShapeDtypeStruct(kv.shape, jnp.float32),
            jax.ShapeDtypeStruct((n_modes, CHUNKS, width), jnp.float32),
        ],
        scratch_shapes=[pltpu.VMEM((n_modes, CHUNKS, lanes), jnp.float32)],
        compiler_params=pltpu.CompilerParams(vmem_limit_bytes=32 * 2**20),
        cost_estimate=pl.CostEstimate(
            flops=6 * kv.size * n_modes, bytes_accessed=8 * kv.size, transcendentals=0
        ),
    )(kv, decay, jump, res)


def run_backward(kv, gl, decay, jump, res, entry):
    steps, _, width = kv.shape
    n_modes = decay.shape[0]
    lanes = math.gcd(width, 128)
    series, row = series_spec(steps, lanes), mode_spec(n_modes, 1, lanes)
    carried = mode_spec(n_modes, CHUNKS, lanes)
    return pl.pallas_call(
        backward_kernel,
        grid=(width // lanes,),
        in_specs=[series, series, row, row, row, carried],
        out_specs=[series, row, row],
        out_shape=[
            jax.ShapeDtypeStruct(kv.shape, jnp.float32),
            jax.ShapeDtypeStruct(decay.shape, jnp.float32),
            jax.ShapeDtypeStruct(decay.shape, jnp.float32),
        ],
        scratch_shapes=[
            pltpu.VMEM((steps, n_modes, CHUNKS, lanes), jnp.float32),
            pltpu.VMEM((n_modes, CHUNKS, lanes), jnp.float32),
            pltpu.VMEM((n_modes, CHUNKS, lanes), jnp.float32),
        ],
        compiler_params=pltpu.CompilerParams(vmem_limit_bytes=44 * 2**20),
        cost_estimate=pl.CostEstimate(
            flops=12 * kv.size * n_modes, bytes_accessed=12 * kv.size, transcendentals=0
        ),
    )(kv, gl, decay, jump, res, entry)


def to_chunks(series):
    length, width = series.shape
    return jnp.swapaxes(series.reshape(CHUNKS, length // CHUNKS, width), 0, 1)


def from_chunks(series):
    steps, _, width = series.shape
    return jnp.swapaxes(series, 0, 1).reshape(CHUNKS * steps, width)


def exchange(blocks, axis):
    devices, index = lax.axis_size(axis), lax.axis_index(axis)
    came = []
    for shift in range(devices):
        target = lax.rem(index + shift, devices)
        block = lax.dynamic_index_in_dim(blocks, target, axis=0, keepdims=False)
        if shift:
            block = lax.ppermute(block, axis, [(i, (i + shift) % devices) for i in range(devices)])
        came.append(block)
    turned = jnp.stack(came[::-1] + came[::-1])
    return lax.dynamic_slice_in_dim(turned, devices - 1 - index, devices, axis=0)


def on_device(out_grad, out_weight, projections, short_filters, residues, decay_rates):
    devices, index = lax.axis_size("ctx"), lax.axis_index("ctx")
    panels = lax.axis_size("fsdp")
    tokens, wide = out_grad.shape
    length = tokens * devices
    share = projections.shape[2] // devices

    series = lax.all_to_all(projections, "ctx", split_axis=2, concat_axis=1, tiled=True)

    rows = tokens // panels
    mine = exchange(out_grad.reshape(panels, rows, wide), "fsdp")
    mine = mine.reshape(panels, rows, -1, wide * panels // devices)
    mine = jnp.transpose(mine, (0, 2, 1, 3)).reshape(devices, rows, -1)
    mine = exchange(mine, "ctx")
    mine = lax.all_gather(mine, "fsdp", axis=1)
    cotangent = mine.reshape(length, -1)

    def own(array):
        return lax.dynamic_slice_in_dim(array, index * share, share, axis=array.ndim - 1)

    filters, res, rates = own(short_filters), own(residues), own(decay_rates)
    taps = filters.shape[1]
    margin = taps - 1
    steps = length // CHUNKS
    decay = jnp.exp(-rates)[:, None, :]
    jump = jnp.exp(-rates * float(steps))[:, None, :]
    res = res[:, None, :]

    extended = jnp.pad(series, ((0, 0), (margin, 0), (0, 0))).astype(jnp.float32)
    delayed = [extended[:, margin - j : margin - j + length, :] for j in range(taps)]
    branches = sum(filters[:, j, None, :] * delayed[j] for j in range(taps))
    q_branch, k_branch, v_branch = branches[0], branches[1], branches[2]
    kv = to_chunks(k_branch * v_branch)
    long_chunks, entry = run_forward(kv, decay, jump, res)
    long_out = from_chunks(long_chunks)
    y_rounded = (q_branch * long_out).astype(jnp.bfloat16)
    y_all = lax.all_gather(y_rounded, "ctx", axis=1, tiled=True)

    outer, side = devices // 2, lax.rem(index, 2)
    paired = out_weight.reshape(out_weight.shape[0], outer, 2, share)

    def half(which):
        columns = lax.dynamic_index_in_dim(paired, which, axis=2, keepdims=False)
        return columns.reshape(-1, outer * share)

    swap = [(i, i ^ 1) for i in range(devices)]
    lanes_of = [[2 * z + x for z in range(outer)] for x in range(2)]
    theirs, ours = half(1 - side), half(side)
    pieces = []
    for piece in jnp.split(cotangent, 2, axis=0):
        sent = jnp.dot(piece, theirs, preferred_element_type=jnp.float32)
        other = lax.ppermute(sent.astype(jnp.bfloat16), "ctx", swap)
        kept = jnp.dot(piece, ours, preferred_element_type=jnp.float32)
        both = (kept + other.astype(jnp.float32)).astype(jnp.bfloat16)
        terms = lax.all_to_all(
            both.reshape(-1, outer, share), "ctx", 1, 0, axis_index_groups=lanes_of
        )
        pieces.append(jnp.sum(terms.astype(jnp.float32), axis=0))
    grad_y = jnp.concatenate(pieces, axis=0)

    grad_weight = lax.dot_general(
        cotangent, y_all, (((0,), (0,)), ((), ())), preferred_element_type=jnp.float32
    ).astype(jnp.bfloat16)

    gkv_chunks, grad_res, grad_rate = run_backward(
        kv, to_chunks(grad_y * q_branch), decay, jump, res, entry
    )
    grad_kv = from_chunks(gkv_chunks)
    grad_branches = jnp.stack([grad_y * long_out, grad_kv * v_branch, grad_kv * k_branch])
    extended_back = jnp.pad(grad_branches, ((0, 0), (0, margin), (0, 0)))
    grad_raw = sum(
        filters[:, j, None, :] * extended_back[:, j : j + length, :] for j in range(taps)
    ).astype(jnp.bfloat16)
    grad_short = jnp.stack(
        [jnp.sum(grad_branches * delayed[j], axis=1) for j in range(taps)], axis=1
    )

    n_short, n_modes = 3 * taps, res.shape[0]
    small = jnp.concatenate(
        [grad_short.reshape(n_short, share), grad_res[:, 0, :], grad_rate[:, 0, :]]
    )
    small = jnp.pad(small, ((0, -small.shape[0] % 16), (0, 0)))
    padded = small.shape[0]
    high = lax.reduce_precision(small, 8, 7)
    parts = jnp.concatenate([high, small - high]).astype(jnp.bfloat16)
    own_rows = 3 * tokens
    sent = jnp.swapaxes(grad_raw.reshape(3, devices, tokens, share), 0, 1)
    sent = jnp.concatenate(
        [
            sent.reshape(devices, own_rows, share),
            jnp.broadcast_to(parts[None], (devices,) + parts.shape),
        ],
        axis=1,
    )
    got = lax.all_to_all(sent, "ctx", 0, 0)
    grad_raw = got[:, :own_rows].reshape(devices, 3, tokens, share)
    grad_raw = jnp.transpose(grad_raw, (1, 2, 0, 3)).reshape(3, tokens, -1)
    low = got[:, own_rows + padded :].astype(jnp.float32)
    small = got[:, own_rows : own_rows + padded].astype(jnp.float32) + low
    small = jnp.swapaxes(small, 0, 1).reshape(padded, -1)
    return (
        grad_weight,
        grad_raw,
        small[:n_short].reshape(3, taps, -1),
        small[n_short : n_short + n_modes],
        small[n_short + n_modes : n_short + 2 * n_modes],
    )


def solution(mesh):
    placed = (
        P("ctx", "fsdp"),
        P("ctx", "fsdp"),
        P(None, "ctx", "fsdp"),
        P(None, None, "fsdp"),
        P(None, "fsdp"),
        P(None, "fsdp"),
    )
    return jax.shard_map(
        on_device,
        mesh=mesh,
        in_specs=placed,
        out_specs=(
            P("ctx", "fsdp"),
            P(None, "ctx", "fsdp"),
            P(None, None, "fsdp"),
            P(None, "fsdp"),
            P(None, "fsdp"),
        ),
        check_vma=False,
    )
```

```python
import math

import jax
import jax.numpy as jnp
from jax import lax
from jax.experimental import pallas as pl
from jax.experimental.pallas import tpu as pltpu
from jax.sharding import PartitionSpec as P

CHUNKS = 8
GROUP = 8


def pair_sum(terms):
    while len(terms) > 1:
        paired = [a + b for a, b in zip(terms[0::2], terms[1::2])]
        terms = paired + ([terms[-1]] if len(terms) % 2 else [])
    return terms[0]


def spread(ref, modes, lanes):
    return [jnp.broadcast_to(ref[n], (CHUNKS, lanes)) for n in modes]


def forward_kernel(kv_ref, decay_ref, jump_ref, res_ref, long_ref, entry_ref, final_ref):
    steps, _, lanes = kv_ref.shape
    modes = range(decay_ref.shape[0])
    decay = spread(decay_ref, modes, lanes)
    zeros = [jnp.zeros((CHUNKS, lanes), jnp.float32) for _ in modes]

    def finals(r, state):
        x = kv_ref[r]
        return [d * s + x for d, s in zip(decay, state)]

    state = lax.fori_loop(0, steps, finals, zeros, unroll=4)
    for n in modes:
        final_ref[n] = state[n]
    jump = jump_ref[...]
    entering = jnp.zeros_like(jump)
    for c in range(CHUNKS):
        entry_ref[:, c : c + 1, :] = entering
        entering = jump * entering + final_ref[:, c : c + 1, :]
    res = spread(res_ref, modes, lanes)

    def outputs(r, state):
        x = kv_ref[r]
        state = [d * s + x for d, s in zip(decay, state)]
        long_ref[r] = pair_sum([w * s for w, s in zip(res, state)])
        return state

    lax.fori_loop(0, steps, outputs, [entry_ref[n] for n in modes], unroll=4)


def backward_kernel(
    kv_ref, gl_ref, decay_ref, jump_ref, res_ref, entry_ref,
    gkv_ref, gres_ref, grate_ref, prev_ref, final_ref, enter_ref,
):
    steps, _, lanes = kv_ref.shape
    n_modes = decay_ref.shape[0]
    modes = range(n_modes)
    decay = spread(decay_ref, modes, lanes)
    zeros = [jnp.zeros((CHUNKS, lanes), jnp.float32) for _ in modes]

    def first(r, carry):
        state, adjoint = carry
        x = kv_ref[r]
        g = gl_ref[steps - 1 - r]
        for n in modes:
            prev_ref[r, n] = state[n]
        return (
            [d * s + x for d, s in zip(decay, state)],
            [d * a + g for d, a in zip(decay, adjoint)],
        )

    _, adjoint = lax.fori_loop(0, steps, first, ([entry_ref[n] for n in modes], zeros), unroll=2)
    for n in modes:
        final_ref[n] = adjoint[n]
    jump = jump_ref[...]
    entering = jnp.zeros_like(jump)
    for c in reversed(range(CHUNKS)):
        enter_ref[:, c : c + 1, :] = entering
        entering = jump * entering + final_ref[:, c : c + 1, :]

    for start in range(0, n_modes, GROUP):
        group = range(start, min(start + GROUP, n_modes))
        d_group = spread(decay_ref, group, lanes)
        r_group = spread(res_ref, group, lanes)
        zero = [jnp.zeros((CHUNKS, lanes), jnp.float32) for _ in group]

        def second(k, carry, start=start, group=group, d_group=d_group, r_group=r_group):
            adjoint, res_sum, rate_sum = carry
            r = steps - 1 - k
            g = gl_ref[r]
            x = kv_ref[r]
            adjoint = [d * a + g for d, a in zip(d_group, adjoint)]
            total = pair_sum([w * a for w, a in zip(r_group, adjoint)])
            gkv_ref[r] = total if start == 0 else gkv_ref[r] + total
            res_sum = [s + a * x for s, a in zip(res_sum, adjoint)]
            rate_sum = [s + a * prev_ref[r, n] for s, a, n in zip(rate_sum, adjoint, group)]
            return adjoint, res_sum, rate_sum

        _, res_sum, rate_sum = lax.fori_loop(
            0, steps, second, ([enter_ref[n] for n in group], zero, zero), unroll=2
        )
        for k, n in enumerate(group):
            gres_ref[n] = jnp.sum(res_sum[k], axis=0, keepdims=True)
            grate_ref[n] = (
                -decay_ref[n] * res_ref[n] * jnp.sum(rate_sum[k], axis=0, keepdims=True)
            )


def series_spec(steps, lanes):
    return pl.BlockSpec((steps, CHUNKS, lanes), lambda b: (0, 0, b))


def mode_spec(n_modes, rows, lanes):
    return pl.BlockSpec((n_modes, rows, lanes), lambda b: (0, 0, b))


def run_forward(kv, decay, jump, res):
    steps, _, width = kv.shape
    n_modes = decay.shape[0]
    lanes = math.gcd(width, 128)
    series, row = series_spec(steps, lanes), mode_spec(n_modes, 1, lanes)
    return pl.pallas_call(
        forward_kernel,
        grid=(width // lanes,),
        in_specs=[series, row, row, row],
        out_specs=[series, mode_spec(n_modes, CHUNKS, lanes)],
        out_shape=[
            jax.ShapeDtypeStruct(kv.shape, jnp.float32),
            jax.ShapeDtypeStruct((n_modes, CHUNKS, width), jnp.float32),
        ],
        scratch_shapes=[pltpu.VMEM((n_modes, CHUNKS, lanes), jnp.float32)],
        compiler_params=pltpu.CompilerParams(vmem_limit_bytes=32 * 2**20),
        cost_estimate=pl.CostEstimate(
            flops=6 * kv.size * n_modes, bytes_accessed=8 * kv.size, transcendentals=0
        ),
    )(kv, decay, jump, res)


def run_backward(kv, gl, decay, jump, res, entry):
    steps, _, width = kv.shape
    n_modes = decay.shape[0]
    lanes = math.gcd(width, 128)
    series, row = series_spec(steps, lanes), mode_spec(n_modes, 1, lanes)
    carried = mode_spec(n_modes, CHUNKS, lanes)
    return pl.pallas_call(
        backward_kernel,
        grid=(width // lanes,),
        in_specs=[series, series, row, row, row, carried],
        out_specs=[series, row, row],
        out_shape=[
            jax.ShapeDtypeStruct(kv.shape, jnp.float32),
            jax.ShapeDtypeStruct(decay.shape, jnp.float32),
            jax.ShapeDtypeStruct(decay.shape, jnp.float32),
        ],
        scratch_shapes=[
            pltpu.VMEM((steps, n_modes, CHUNKS, lanes), jnp.float32),
            pltpu.VMEM((n_modes, CHUNKS, lanes), jnp.float32),
            pltpu.VMEM((n_modes, CHUNKS, lanes), jnp.float32),
        ],
        compiler_params=pltpu.CompilerParams(vmem_limit_bytes=44 * 2**20),
        cost_estimate=pl.CostEstimate(
            flops=12 * kv.size * n_modes, bytes_accessed=12 * kv.size, transcendentals=0
        ),
    )(kv, gl, decay, jump, res, entry)


def to_chunks(series):
    length, width = series.shape
    return jnp.swapaxes(series.reshape(CHUNKS, length // CHUNKS, width), 0, 1)


def from_chunks(series):
    steps, _, width = series.shape
    return jnp.swapaxes(series, 0, 1).reshape(CHUNKS * steps, width)


def exchange(blocks, axis):
    devices, index = lax.axis_size(axis), lax.axis_index(axis)
    came = []
    for shift in range(devices):
        target = lax.rem(index + shift, devices)
        block = lax.dynamic_index_in_dim(blocks, target, axis=0, keepdims=False)
        if shift:
            block = lax.ppermute(block, axis, [(i, (i + shift) % devices) for i in range(devices)])
        came.append(block)
    turned = jnp.stack(came[::-1] + came[::-1])
    return lax.dynamic_slice_in_dim(turned, devices - 1 - index, devices, axis=0)


def on_device(out_grad, out_weight, projections, short_filters, residues, decay_rates):
    devices, index = lax.axis_size("ctx"), lax.axis_index("ctx")
    panels = lax.axis_size("fsdp")
    tokens, wide = out_grad.shape
    length = tokens * devices
    share = projections.shape[2] // devices

    series = lax.all_to_all(projections, "ctx", split_axis=2, concat_axis=1, tiled=True)

    rows = tokens // panels
    mine = exchange(out_grad.reshape(panels, rows, wide), "fsdp")
    mine = mine.reshape(panels, rows, -1, wide * panels // devices)
    mine = jnp.transpose(mine, (0, 2, 1, 3)).reshape(devices, rows, -1)
    mine = exchange(mine, "ctx")
    mine = lax.all_gather(mine, "fsdp", axis=1)
    cotangent, series = lax.optimization_barrier((mine.reshape(length, -1), series))

    def own(array):
        return lax.dynamic_slice_in_dim(array, index * share, share, axis=array.ndim - 1)

    filters, res, rates = own(short_filters), own(residues), own(decay_rates)
    taps = filters.shape[1]
    margin = taps - 1
    steps = length // CHUNKS
    decay = jnp.exp(-rates)[:, None, :]
    jump = jnp.exp(-rates * float(steps))[:, None, :]
    res = res[:, None, :]

    extended = jnp.pad(series, ((0, 0), (margin, 0), (0, 0))).astype(jnp.float32)
    delayed = [extended[:, margin - j : margin - j + length, :] for j in range(taps)]
    branches = sum(filters[:, j, None, :] * delayed[j] for j in range(taps))
    q_branch, k_branch, v_branch = branches[0], branches[1], branches[2]
    kv = to_chunks(k_branch * v_branch)
    long_chunks, entry = run_forward(kv, decay, jump, res)
    long_out = from_chunks(long_chunks)
    y_rounded = (q_branch * long_out).astype(jnp.bfloat16)
    outer, side = devices // 2, lax.rem(index, 2)
    paired = out_weight.reshape(out_weight.shape[0], outer, 2, share)

    def half(which):
        columns = lax.dynamic_index_in_dim(paired, which, axis=2, keepdims=False)
        return columns.reshape(-1, outer * share)

    swap = [(i, i ^ 1) for i in range(devices)]
    lanes_of = [[2 * z + x for z in range(outer)] for x in range(2)]
    theirs, ours = half(1 - side), half(side)
    pieces = []
    for piece in jnp.split(cotangent, 2, axis=0):
        sent = jnp.dot(piece, theirs, preferred_element_type=jnp.float32)
        other = lax.ppermute(sent.astype(jnp.bfloat16), "ctx", swap)
        kept = jnp.dot(piece, ours, preferred_element_type=jnp.float32)
        both = (kept + other.astype(jnp.float32)).astype(jnp.bfloat16)
        both, y_rounded = lax.optimization_barrier((both, y_rounded))
        terms = lax.all_to_all(
            both.reshape(-1, outer, share), "ctx", 1, 0, axis_index_groups=lanes_of
        )
        if not pieces:
            y_all = lax.all_gather(y_rounded, "ctx", axis=1, tiled=True)
        pieces.append(jnp.sum(terms.astype(jnp.float32), axis=0))
    grad_y = jnp.concatenate(pieces, axis=0)

    grad_weight = lax.dot_general(
        cotangent, y_all, (((0,), (0,)), ((), ())), preferred_element_type=jnp.float32
    ).astype(jnp.bfloat16)

    gkv_chunks, grad_res, grad_rate = run_backward(
        kv, to_chunks(grad_y * q_branch), decay, jump, res, entry
    )
    grad_kv = from_chunks(gkv_chunks)
    grad_branches = jnp.stack([grad_y * long_out, grad_kv * v_branch, grad_kv * k_branch])
    extended_back = jnp.pad(grad_branches, ((0, 0), (0, margin), (0, 0)))
    grad_raw = sum(
        filters[:, j, None, :] * extended_back[:, j : j + length, :] for j in range(taps)
    ).astype(jnp.bfloat16)
    grad_short = jnp.stack(
        [jnp.sum(grad_branches * delayed[j], axis=1) for j in range(taps)], axis=1
    )

    n_short, n_modes = 3 * taps, res.shape[0]
    small = jnp.concatenate(
        [grad_short.reshape(n_short, share), grad_res[:, 0, :], grad_rate[:, 0, :]]
    )
    small = jnp.pad(small, ((0, -small.shape[0] % 16), (0, 0)))
    padded = small.shape[0]
    high = lax.reduce_precision(small, 8, 7)
    parts = jnp.concatenate([high, small - high]).astype(jnp.bfloat16)
    own_rows = 3 * tokens
    sent = jnp.swapaxes(grad_raw.reshape(3, devices, tokens, share), 0, 1)
    sent = jnp.concatenate(
        [
            sent.reshape(devices, own_rows, share),
            jnp.broadcast_to(parts[None], (devices,) + parts.shape),
        ],
        axis=1,
    )
    got = lax.all_to_all(sent, "ctx", 0, 0)
    grad_raw = got[:, :own_rows].reshape(devices, 3, tokens, share)
    grad_raw = jnp.transpose(grad_raw, (1, 2, 0, 3)).reshape(3, tokens, -1)
    low = got[:, own_rows + padded :].astype(jnp.float32)
    small = got[:, own_rows : own_rows + padded].astype(jnp.float32) + low
    small = jnp.swapaxes(small, 0, 1).reshape(padded, -1)
    return (
        grad_weight,
        grad_raw,
        small[:n_short].reshape(3, taps, -1),
        small[n_short : n_short + n_modes],
        small[n_short + n_modes : n_short + 2 * n_modes],
    )


def solution(mesh):
    placed = (
        P("ctx", "fsdp"),
        P("ctx", "fsdp"),
        P(None, "ctx", "fsdp"),
        P(None, None, "fsdp"),
        P(None, "fsdp"),
        P(None, "fsdp"),
    )
    return jax.shard_map(
        on_device,
        mesh=mesh,
        in_specs=placed,
        out_specs=(
            P("ctx", "fsdp"),
            P(None, "ctx", "fsdp"),
            P(None, None, "fsdp"),
            P(None, "fsdp"),
            P(None, "fsdp"),
        ),
        check_vma=False,
    )
```
